512 devices in a mesh: replica: 64 (over y, z_hi, x, core), dp: 8 (over z_lo).
Axes of the slice: x: 4, y: 4, z: 16 (z_hi: 2, z_lo: 8; z = z_hi * 8 + z_lo), core: 2. Of those that a mesh axis runs over, the one named last changes fastest.
Arguments:
- local_weight: float32 [2048, 8192], P(('replica', 'dp')), may hold values from -6 to 6
- adam_first: float32 [2048, 8192], P(('replica', 'dp')), may hold values from -6 to 6
- adam_second: float32 [2048, 8192], P(('replica', 'dp')), may hold values from 0.05 to 2
- hidden_acts: bfloat16 [2, 32, 65536], P(None, None, ('replica', 'dp')), may hold values from -6 to 6
- out_grads: bfloat16 [2, 65536, 8192], P(None, ('replica', 'dp')), may hold values from -0.4375 to 0.4375
- global_weight: float32 [32, 8192], P('dp', 'replica'), may hold values from -6 to 6
- outer_momentum: float32 [32, 8192], P('dp', 'replica'), may hold values from -6 to 6
Outputs:
- new_local: float32 [2048, 8192], P(('replica', 'dp'))
- new_first: float32 [2048, 8192], P(('replica', 'dp'))
- new_second: float32 [2048, 8192], P(('replica', 'dp'))
- new_global: float32 [32, 8192], P('dp', 'replica')
- new_momentum: float32 [32, 8192], P('dp', 'replica')
The draws below stay inside these ranges and needn't reach their ends.
All inputs are finite; a program needn't handle non-finite values.
Results may differ from the reference program's by a relative error of at most 0.0003.
Values sent between devices are 32-bit elements; how exact they have to be, the bound alone decides.
No kernel may reach another device: no remote copies, remote signals or barrier semaphores. Data moves between devices by JAX's collectives and lax.ppermute only.
A program may use at most 64 MiB of HBM per device.

```python
import math
import jax
import jax.numpy as jnp
from jax import lax

D = 8192
TOK_DEV = 128
ITERS = 2
ROWS = 32
LOCAL_ROWS = 2048
TOKENS = 65536
N_REPLICA = 64
N_DP = 8


def levels(stream_key, dims, cuts, smallest, largest):
    gain = 1.0
    for position, blocks in cuts:
        steps = jax.random.uniform(jax.random.fold_in(jax.random.fold_in(stream_key, 6), position), (blocks,), jnp.float32, smallest / len(cuts), largest / len(cuts))
        gain = gain * jnp.repeat(jnp.exp(steps), dims[position] // blocks).reshape((-1,) + (1,) * (len(dims) - 1 - position))
    return gain


def noise(key, dims, spread, most, pieces=(), held_as=jnp.bfloat16):
    gain = levels(key, dims, pieces, -0.22, 0.18) if pieces else 1.0
    result = jax.random.normal(key, dims, jnp.float32) * spread * gain
    return jnp.minimum(jnp.maximum(result, -most), most).astype(held_as)


def setup_inputs(seed: int = 0) -> dict:
    splits = jax.random.split(jax.random.key(seed), 8)
    return {
        "local_weight": noise(splits[0], (LOCAL_ROWS, D), 1.0, 6.0, ((0, 512),), jnp.float32),
        "adam_first": noise(splits[1], (LOCAL_ROWS, D), 0.5, 6.0, ((0, 512),), jnp.float32),
        "adam_second": jnp.clip(jnp.exp(math.log(2.0) - 3.6888794 * jax.random.uniform(splits[2], (LOCAL_ROWS, D), jnp.float32) ** levels(splits[2], (LOCAL_ROWS, D), ((0, 512),), -0.2, 0.2)), 0.05, 2.0),
        "hidden_acts": noise(splits[3], (ITERS, ROWS, TOKENS), 1.0, 6.0, ((2, 512),)),
        "out_grads": noise(splits[4], (ITERS, TOKENS, D), 0.03, 0.4375, ((1, 512),)),
        "global_weight": noise(splits[5], (ROWS, D), 1.0, 6.0, ((0, 8), (1, 64)), jnp.float32),
        "outer_momentum": noise(splits[6], (ROWS, D), 0.5, 6.0, ((0, 8), (1, 64)), jnp.float32),
    }


beta_one = 0.9
beta_two = 0.95
inner_rate = 0.02
decay_rate = 0.1
tiny_eps = 1e-08
outer_rate = 0.7
outer_beta = 0.9
mix_share = 0.5

def reference(local_weight, adam_first, adam_second, hidden_acts, out_grads, global_weight, outer_momentum):
    weights = local_weight.reshape(N_REPLICA, ROWS, D)
    firsts = adam_first.reshape(N_REPLICA, ROWS, D)
    seconds = adam_second.reshape(N_REPLICA, ROWS, D)
    activations = hidden_acts.reshape(ITERS, ROWS, N_REPLICA, N_DP, TOK_DEV)
    errors = out_grads.reshape(ITERS, N_REPLICA, N_DP, TOK_DEV, D)

    def one_replica(index):
        weight = weights[index]
        first_moment = firsts[index]
        second_moment = seconds[index]
        for inner_step in range(ITERS):
            left = activations[inner_step][:, index].astype(jnp.float32)
            right = errors[inner_step][index].astype(jnp.float32)
            partials = jnp.einsum('rnt,ntd->nrd', left, right)
            gradient = lax.optimization_barrier(jnp.sum(partials, axis=0))
            first_moment = beta_one * first_moment + (1.0 - beta_one) * gradient
            second_moment = beta_two * second_moment + (1.0 - beta_two) * gradient * gradient
            update = first_moment / (jnp.sqrt(second_moment) + tiny_eps)
            weight = weight - inner_rate * (update + decay_rate * weight)
        return (weight, first_moment, second_moment)
    trained, new_first, new_second = lax.map(one_replica, jnp.arange(N_REPLICA, dtype=jnp.int32))
    average = lax.optimization_barrier(jnp.sum(trained, axis=0)) / N_REPLICA
    delta = global_weight - average
    new_momentum = outer_beta * outer_momentum + delta
    new_global = global_weight - outer_rate * (delta + outer_beta * new_momentum)
    new_local = mix_share * trained + (1.0 - mix_share) * new_global[None]
    return (new_local.reshape(LOCAL_ROWS, D), new_first.reshape(LOCAL_ROWS, D), new_second.reshape(LOCAL_ROWS, D), new_global, new_momentum)
```

```python
import jax
import jax.numpy as jnp
from jax import lax
from jax.sharding import PartitionSpec as P

beta_one = 0.9
beta_two = 0.95
inner_rate = 0.02
decay_rate = 0.1
tiny_eps = 1e-08
outer_rate = 0.7
outer_beta = 0.9
mix_share = 0.5


def body(
    local_weight, adam_first, adam_second, hidden_acts, out_grads, global_weight, outer_momentum
):
    replicas = lax.axis_size("replica")
    rings = lax.axis_size("dp")
    steps_count, rows, tokens = hidden_acts.shape
    row_total = rows // rings
    columns = out_grads.shape[2]
    ordered = hidden_acts.reshape(steps_count, rings, row_total, tokens).transpose(1, 0, 2, 3)
    blocks = [
        jnp.pad(ordered[:, k : k + 1], ((0, 0), (0, 0), (0, 0), (k * tokens, (steps_count - 1 - k) * tokens)))
        for k in range(steps_count)
    ]
    left = jnp.concatenate(blocks, axis=1).reshape(rings * steps_count * row_total, steps_count * tokens)
    right = out_grads.reshape(steps_count * tokens, columns)
    partials = jnp.dot(left, right, preferred_element_type=jnp.float32)
    summed = lax.psum_scatter(
        partials.reshape(rings, steps_count * row_total, columns), "dp", scatter_dimension=0, tiled=False
    )
    weight = local_weight
    first_moment = adam_first
    second_moment = adam_second
    for k in range(steps_count):
        gradient = summed[k * row_total : (k + 1) * row_total]
        first_moment = beta_one * first_moment + (1.0 - beta_one) * gradient
        second_moment = beta_two * second_moment + (1.0 - beta_two) * gradient * gradient
        update = first_moment / (jnp.sqrt(second_moment) + tiny_eps)
        weight = weight - inner_rate * (update + decay_rate * weight)
    width = columns // replicas
    parts = weight.reshape(row_total, replicas, width).transpose(1, 0, 2)
    parts = lax.all_to_all(parts, "replica", 0, 0, tiled=True)
    average = jnp.sum(parts, axis=0) / replicas
    delta = global_weight - average
    new_momentum = outer_beta * outer_momentum + delta
    new_global = global_weight - outer_rate * (delta + outer_beta * new_momentum)
    copies = jnp.broadcast_to(new_global[None], (replicas, row_total, width))
    gathered = lax.all_to_all(copies, "replica", 0, 0, tiled=True)
    gathered = gathered.transpose(1, 0, 2).reshape(row_total, columns)
    new_local = mix_share * weight + (1.0 - mix_share) * gathered
    return (new_local, first_moment, second_moment, new_global, new_momentum)


def solution(mesh):
    placed = (
        P(("replica", "dp"), None),
        P(("replica", "dp"), None),
        P(("replica", "dp"), None),
        P(None, None, ("replica", "dp")),
        P(None, ("replica", "dp"), None),
        P("dp", "replica"),
        P("dp", "replica"),
    )
    return jax.shard_map(
        body,
        mesh=mesh,
        in_specs=placed,
        out_specs=(
            P(("replica", "dp"), None),
            P(("replica", "dp"), None),
            P(("replica", "dp"), None),
            P("dp", "replica"),
            P("dp", "replica"),
        ),
        check_vma=False,
    )
```

```python
import jax
import jax.numpy as jnp
from jax import lax
from jax.sharding import Mesh
from jax.sharding import PartitionSpec as P

beta_one = 0.9
beta_two = 0.95
inner_rate = 0.02
decay_rate = 0.1
tiny_eps = 1e-08
outer_rate = 0.7
outer_beta = 0.9
mix_share = 0.5

REPLICA_PARTS = {"y": 4, "far": 2, "x": 4, "core": 2}
OUTER = ("y", "far")
INNER = ("x", "core")
LANES = 128


def pick(parts, index):
    return lax.dynamic_index_in_dim(parts, index, 0, keepdims=False)


def reduce_line(parts):
    size = lax.axis_size("dp")
    place = lax.axis_index("dp")
    at = lambda shift: pick(parts, lax.rem(place + shift + 2 * size, size))
    last = size - 2
    up = down = up_sent = down_sent = up_near = down_near = None
    for step in range(1, last + 1):
        hop = 1 if step < last else 2
        count = step if step < last else size - 2
        up_sent = at(-step if step < last else 2)
        if up is not None:
            up, _ = lax.optimization_barrier((up, down_sent))
            up_sent = up_sent + up
        up = lax.ppermute(up_sent, "dp", [(k, k + hop) for k in range(count)])
        down_sent = at(step if step < last else -2)
        if down is not None:
            down, _ = lax.optimization_barrier((down, up_sent))
            down_sent = down_sent + down
        down = lax.ppermute(
            down_sent, "dp", [(size - 1 - k, size - 1 - k - hop) for k in range(count)]
        )
        if step == 1:
            up_own, down_own, up_sent, down_sent = lax.optimization_barrier((at(1), at(-1), up_sent, down_sent))
            up_near = lax.ppermute(up_own, "dp", [(k, k + 1) for k in range(size - 1)])
            down_near = lax.ppermute(down_own, "dp", [(k + 1, k) for k in range(size - 1)])
    return (up + down) + (up_near + down_near) + at(0)


def copies(block, count):
    return jnp.broadcast_to(block[None], (count,) + block.shape)


def body(
    local_weight, adam_first, adam_second, hidden_acts, out_grads, global_weight, outer_momentum
):
    replicas = 1
    for size in REPLICA_PARTS.values():
        replicas *= size
    inner = REPLICA_PARTS["x"] * REPLICA_PARTS["core"]
    outer = replicas // inner
    rings = lax.axis_size("dp")
    steps_count, rows, tokens = hidden_acts.shape
    row_total = rows // rings
    columns = out_grads.shape[2]
    ordered = hidden_acts.reshape(steps_count, rings, row_total, tokens).transpose(1, 0, 2, 3)
    blocks = [
        jnp.pad(
            ordered[:, k : k + 1],
            ((0, 0), (0, 0), (0, 0), (k * tokens, (steps_count - 1 - k) * tokens)),
        )
        for k in range(steps_count)
    ]
    left = jnp.concatenate(blocks, axis=1)
    left = left.reshape(rings * steps_count * row_total, steps_count * tokens)
    right = out_grads.reshape(steps_count * tokens, columns)
    partials = jnp.dot(left, right, preferred_element_type=jnp.float32)
    summed = reduce_line(partials.reshape(rings, steps_count * row_total, columns))

    weight = local_weight
    first_moment = adam_first
    second_moment = adam_second
    for k in range(steps_count):
        gradient = summed[k * row_total : (k + 1) * row_total]
        first_moment = beta_one * first_moment + (1.0 - beta_one) * gradient
        second_moment = beta_two * second_moment + (1.0 - beta_two) * gradient * gradient
        update = first_moment / (jnp.sqrt(second_moment) + tiny_eps)
        weight = weight - inner_rate * (update + decay_rate * weight)

    pull = outer_rate * (1.0 + outer_beta)
    still = global_weight - pull * global_weight - outer_rate * outer_beta * outer_beta * outer_momentum
    slot = lax.axis_index(OUTER)
    parts = weight.reshape(row_total, outer, inner, LANES).transpose(2, 1, 0, 3)
    parts, still, slot = lax.optimization_barrier((parts, still, slot))
    parts = lax.all_to_all(parts, INNER, 0, 0, tiled=True)
    share = jnp.sum(parts, axis=0) * (pull / replicas)
    mine = lax.broadcasted_iota(jnp.int32, share.shape, 0) == slot
    share = share + jnp.where(mine, still[None], 0.0)
    shares = lax.all_to_all(copies(share, outer), OUTER, 0, 0, tiled=True)
    known = jnp.sum(shares, axis=0)
    gathered = lax.all_to_all(copies(known, inner), INNER, 0, 0, tiled=True)
    gathered, known, slot = lax.optimization_barrier((gathered, known, slot))
    gathered = gathered.transpose(2, 1, 0, 3).reshape(row_total, columns)
    new_local = mix_share * weight + (1.0 - mix_share) * gathered
    new_global = pick(known, slot)
    average = (new_global - still) * (1.0 / pull)
    new_momentum = outer_beta * outer_momentum + (global_weight - average)
    return (new_local, first_moment, second_moment, new_global, new_momentum)


def solution(mesh):
    sizes = tuple(REPLICA_PARTS.values()) + (mesh.shape["dp"],)
    fine = Mesh(mesh.devices.reshape(sizes), tuple(REPLICA_PARTS) + ("dp",))
    replica = tuple(REPLICA_PARTS)
    stacked = P(replica + ("dp",), None)
    held = P("dp", replica)
    return jax.shard_map(
        body,
        mesh=fine,
        in_specs=(
            stacked,
            stacked,
            stacked,
            P(None, None, replica + ("dp",)),
            P(None, replica + ("dp",), None),
            held,
            held,
        ),
        out_specs=(stacked, stacked, stacked, held, held),
        check_vma=False,
    )
```

```python
import jax
import jax.numpy as jnp
from jax import lax
from jax.sharding import Mesh
from jax.sharding import PartitionSpec as P

beta_one = 0.9
beta_two = 0.95
inner_rate = 0.02
decay_rate = 0.1
tiny_eps = 1e-08
outer_rate = 0.7
outer_beta = 0.9
mix_share = 0.5

REPLICA_PARTS = {"y": 4, "far": 2, "x": 4, "core": 2}
OUTER = ("y", "far")
INNER = ("x", "core")
LANES = 128


def pick(parts, index):
    return lax.dynamic_index_in_dim(parts, index, 0, keepdims=False)


def reduce_line(parts):
    size = lax.axis_size("dp")
    place = lax.axis_index("dp")
    at = lambda shift: pick(parts, lax.rem(place + shift + 2 * size, size))
    end = size - 1
    last = size - 2
    rights = [(k, k + 1) for k in range(end)]
    lefts = [(k + 1, k) for k in range(end)]
    up_sent = at(jnp.where(place == 0, end, 1))
    down_sent = at(jnp.where(place == end, -end, -1))
    up = lax.ppermute(up_sent, "dp", rights)
    down = lax.ppermute(down_sent, "dp", lefts)
    near = jnp.where(place >= 2, up, 0.0) + jnp.where(place <= end - 2, down, 0.0)
    own = at(0) + near
    for step in range(2, last):
        up, _ = lax.optimization_barrier((up, down_sent))
        up_sent = at(-step) + up
        if step == 4:
            up_sent, own = lax.optimization_barrier((up_sent, own))
        up = lax.ppermute(up_sent, "dp", [(k, k + 1) for k in range(step)])
        down, _ = lax.optimization_barrier((down, up_sent))
        down_sent = at(step) + down
        down = lax.ppermute(down_sent, "dp", [(end - k, end - k - 1) for k in range(step)])
    up, _ = lax.optimization_barrier((up, down_sent))
    up_sent = at(2) + up
    up = lax.ppermute(up_sent, "dp", [(k, k + 2) for k in range(last)])
    down, _ = lax.optimization_barrier((down, up_sent))
    down_sent = at(-2) + down
    down = lax.ppermute(down_sent, "dp", [(k + 2, k) for k in range(last)])
    edge = at(jnp.where(place == 0, 1, -1))
    edge, _ = lax.optimization_barrier((edge, down_sent))
    edge = lax.ppermute(edge, "dp", [(0, 1), (end, end - 1)])
    return (up + down) + (own + edge)


def copies(block, count):
    return jnp.broadcast_to(block[None], (count,) + block.shape)


def body(
    local_weight, adam_first, adam_second, hidden_acts, out_grads, global_weight, outer_momentum
):
    replicas = 1
    for size in REPLICA_PARTS.values():
        replicas *= size
    inner = REPLICA_PARTS["x"] * REPLICA_PARTS["core"]
    outer = replicas // inner
    rings = lax.axis_size("dp")
    steps_count, rows, tokens = hidden_acts.shape
    row_total = rows // rings
    columns = out_grads.shape[2]
    ordered = hidden_acts.reshape(steps_count, rings, row_total, tokens).transpose(1, 0, 2, 3)
    blocks = [
        jnp.pad(
            ordered[:, k : k + 1],
            ((0, 0), (0, 0), (0, 0), (k * tokens, (steps_count - 1 - k) * tokens)),
        )
        for k in range(steps_count)
    ]
    left = jnp.concatenate(blocks, axis=1)
    left = left.reshape(rings * steps_count * row_total, steps_count * tokens)
    right = out_grads.reshape(steps_count * tokens, columns)
    partials = jnp.dot(left, right, preferred_element_type=jnp.float32)
    summed = reduce_line(partials.reshape(rings, steps_count * row_total, columns))

    weight = local_weight
    first_moment = adam_first
    second_moment = adam_second
    for k in range(steps_count):
        gradient = summed[k * row_total : (k + 1) * row_total]
        first_moment = beta_one * first_moment + (1.0 - beta_one) * gradient
        second_moment = beta_two * second_moment + (1.0 - beta_two) * gradient * gradient
        update = first_moment / (jnp.sqrt(second_moment) + tiny_eps)
        weight = weight - inner_rate * (update + decay_rate * weight)

    pull = outer_rate * (1.0 + outer_beta)
    still = global_weight - pull * global_weight - outer_rate * outer_beta * outer_beta * outer_momentum
    slot = lax.axis_index(OUTER)
    parts = weight.reshape(row_total, outer, inner, LANES).transpose(2, 1, 0, 3)
    mine = lax.broadcasted_iota(jnp.int32, parts.shape[1:], 0) == slot
    added = jnp.where(mine, still[None], 0.0)
    parts, added, still, slot = lax.optimization_barrier((parts, added, still, slot))
    parts = lax.all_to_all(parts, INNER, 0, 0, tiled=True)
    share = jnp.sum(parts, axis=0) * (pull / replicas) + added
    shares = lax.all_to_all(copies(share, outer), OUTER, 0, 0, tiled=True)
    known = jnp.sum(shares, axis=0)
    gathered = lax.all_to_all(copies(known, inner), INNER, 0, 0, tiled=True)
    gathered, known, slot = lax.optimization_barrier((gathered, known, slot))
    gathered = gathered.transpose(2, 1, 0, 3).reshape(row_total, columns)
    new_local = mix_share * weight + (1.0 - mix_share) * gathered
    new_global = pick(known, slot)
    average = (new_global - still) * (1.0 / pull)
    new_momentum = outer_beta * outer_momentum + (global_weight - average)
    return (new_local, first_moment, second_moment, new_global, new_momentum)


def solution(mesh):
    sizes = tuple(REPLICA_PARTS.values()) + (mesh.shape["dp"],)
    fine = Mesh(mesh.devices.reshape(sizes), tuple(REPLICA_PARTS) + ("dp",))
    replica = tuple(REPLICA_PARTS)
    stacked = P(replica + ("dp",), None)
    held = P("dp", replica)
    return jax.shard_map(
        body,
        mesh=fine,
        in_specs=(
            stacked,
            stacked,
            stacked,
            P(None, None, replica + ("dp",)),
            P(None, replica + ("dp",), None),
            held,
            held,
        ),
        out_specs=(stacked, stacked, stacked, held, held),
        check_vma=False,
    )
```

```python
import jax
import jax.numpy as jnp
from jax import lax
from jax.sharding import Mesh
from jax.sharding import PartitionSpec as P

beta_one = 0.9
beta_two = 0.95
inner_rate = 0.02
decay_rate = 0.1
tiny_eps = 1e-08
outer_rate = 0.7
outer_beta = 0.9
mix_share = 0.5

REPLICA_PARTS = {"y": 4, "far": 2, "x": 4, "core": 2}
OUTER = ("y", "far")
INNER = ("x", "core")
LANES = 128


def pick(parts, index):
    return lax.dynamic_index_in_dim(parts, index, 0, keepdims=False)


def reduce_line(parts):
    size = lax.axis_size("dp")
    place = lax.axis_index("dp")
    at = lambda shift: pick(parts, lax.rem(place + shift + 2 * size, size))
    end = size - 1
    last = size - 2
    rights = [(k, k + 1) for k in range(end)]
    lefts = [(k + 1, k) for k in range(end)]
    up_sent = at(jnp.where(place == 0, end, 1))
    down_sent = at(jnp.where(place == end, -end, -1))
    up = lax.ppermute(up_sent, "dp", rights)
    down = lax.ppermute(down_sent, "dp", lefts)
    near = jnp.where(place >= 2, up, 0.0) + jnp.where(place <= end - 2, down, 0.0)
    own = at(0) + near
    for step in range(2, last):
        up, _ = lax.optimization_barrier((up, down_sent))
        up_sent = at(-step) + up
        if step == 4:
            up_sent, own = lax.optimization_barrier((up_sent, own))
        up = lax.ppermute(up_sent, "dp", [(k, k + 1) for k in range(step)])
        down, _ = lax.optimization_barrier((down, up_sent))
        down_sent = at(step) + down
        down = lax.ppermute(down_sent, "dp", [(end - k, end - k - 1) for k in range(step)])
    up, _ = lax.optimization_barrier((up, down_sent))
    up_sent = at(2) + up
    up = lax.ppermute(up_sent, "dp", [(k, k + 2) for k in range(last)])
    down, _ = lax.optimization_barrier((down, up_sent))
    down_sent = at(-2) + down
    down = lax.ppermute(down_sent, "dp", [(k + 2, k) for k in range(last)])
    edge = at(jnp.where(place == 0, 1, -1))
    edge, _ = lax.optimization_barrier((edge, down_sent))
    edge = lax.ppermute(edge, "dp", [(0, 1), (end, end - 1)])
    return (up + down) + (own + edge)


def copies(block, count):
    return jnp.broadcast_to(block[None], (count,) + block.shape)


def body(
    local_weight, adam_first, adam_second, hidden_acts, out_grads, global_weight, outer_momentum
):
    replicas = 1
    for size in REPLICA_PARTS.values():
        replicas *= size
    inner = REPLICA_PARTS["x"] * REPLICA_PARTS["core"]
    outer = replicas // inner
    rings = lax.axis_size("dp")
    steps_count, rows, tokens = hidden_acts.shape
    row_total = rows // rings
    columns = out_grads.shape[2]
    ordered = hidden_acts.reshape(steps_count, rings, row_total, tokens).transpose(1, 0, 2, 3)
    blocks = [
        jnp.pad(
            ordered[:, k : k + 1],
            ((0, 0), (0, 0), (0, 0), (k * tokens, (steps_count - 1 - k) * tokens)),
        )
        for k in range(steps_count)
    ]
    left = jnp.concatenate(blocks, axis=1)
    left = left.reshape(rings * steps_count * row_total, steps_count * tokens)
    right = out_grads.reshape(steps_count * tokens, columns)
    partials = jnp.dot(left, right, preferred_element_type=jnp.float32)
    summed = reduce_line(partials.reshape(rings, steps_count * row_total, columns))

    weight = local_weight
    first_moment = adam_first
    second_moment = adam_second
    for k in range(steps_count):
        gradient = summed[k * row_total : (k + 1) * row_total]
        first_moment = beta_one * first_moment + (1.0 - beta_one) * gradient
        second_moment = beta_two * second_moment + (1.0 - beta_two) * gradient * gradient
        update = first_moment / (jnp.sqrt(second_moment) + tiny_eps)
        weight = weight - inner_rate * (update + decay_rate * weight)

    pull = outer_rate * (1.0 + outer_beta)
    still = global_weight - pull * global_weight - outer_rate * outer_beta * outer_beta * outer_momentum
    far = lax.axis_index("far")
    sides = REPLICA_PARTS["far"]
    lines = REPLICA_PARTS["y"]
    parts = weight.reshape(row_total, lines, sides, inner, LANES).transpose(1, 3, 2, 0, 4)
    parts = parts.reshape((lines * inner, sides) + still.shape)
    mine = lax.broadcasted_iota(jnp.int32, parts.shape[1:], 0) == far
    added = jnp.where(mine, still[None], 0.0)
    parts, added, still, far = lax.optimization_barrier((parts, added, still, far))
    parts = lax.all_to_all(parts, ("y", "x", "core"), 0, 0, tiled=True)
    share = jnp.sum(parts, axis=0) * (pull / replicas) + added
    second = lax.ppermute(share, "far", [(0, 1)])
    first = lax.ppermute(share, "far", [(1, 0)])
    known = (share + second) + first
    gathered = lax.all_to_all(copies(known, lines * inner), ("y", "x", "core"), 0, 0, tiled=True)
    gathered, known, far = lax.optimization_barrier((gathered, known, far))
    gathered = gathered.reshape((lines, inner, sides) + still.shape)
    gathered = gathered.transpose(3, 0, 2, 1, 4).reshape(row_total, columns)
    new_local = mix_share * weight + (1.0 - mix_share) * gathered
    new_global = pick(known, far)
    average = (new_global - still) * (1.0 / pull)
    new_momentum = outer_beta * outer_momentum + (global_weight - average)
    return (new_local, first_moment, second_moment, new_global, new_momentum)


def solution(mesh):
    sizes = tuple(REPLICA_PARTS.values()) + (mesh.shape["dp"],)
    fine = Mesh(mesh.devices.reshape(sizes), tuple(REPLICA_PARTS) + ("dp",))
    replica = tuple(REPLICA_PARTS)
    stacked = P(replica + ("dp",), None)
    held = P("dp", replica)
    return jax.shard_map(
        body,
        mesh=fine,
        in_specs=(
            stacked,
            stacked,
            stacked,
            P(None, None, replica + ("dp",)),
            P(None, replica + ("dp",), None),
            held,
            held,
        ),
        out_specs=(stacked, stacked, stacked, held, held),
        check_vma=False,
    )
```

```python
import functools

import jax
import jax.numpy as jnp
from jax import lax
from jax.experimental import pallas as pl
from jax.experimental.pallas import tpu as pltpu
from jax.sharding import Mesh
from jax.sharding import PartitionSpec as P

beta_one = 0.9
beta_two = 0.95
inner_rate = 0.02
decay_rate = 0.1
tiny_eps = 1e-08
outer_rate = 0.7
outer_beta = 0.9
mix_share = 0.5

REPLICA_PARTS = {"y": 4, "far": 2, "x": 4, "core": 2}
OUTER = ("y", "far")
INNER = ("x", "core")
LANES = 128


def pick(parts, index):
    return lax.dynamic_index_in_dim(parts, index, 0, keepdims=False)


CHUNKS = 2


def partial_kernel(rings, hidden_hbm, grads_hbm, out_ref, hidden, grads, hidden_sem, grads_sem):
    steps, rows, tokens = hidden.shape
    width = grads.shape[3]
    held = rows // rings
    group = steps * held
    total = rings * group
    hidden_copy = pltpu.make_async_copy(hidden_hbm, hidden, hidden_sem)
    hidden_copy.start()
    fetches = []
    for part in range(CHUNKS):
        fetch = pltpu.make_async_copy(
            grads_hbm.at[:, :, pl.ds(part * width, width)], grads.at[part], grads_sem.at[part]
        )
        fetch.start()
        fetches.append(fetch)
    place = lax.broadcasted_iota(jnp.int32, (total, rows), 0)
    source = lax.broadcasted_iota(jnp.int32, (total, rows), 1)
    choices = []
    for k in range(steps):
        wanted = (place // group) * held + place % group - k * held
        chosen = (source == wanted) & ((place % group) // held == k)
        choices.append(jnp.where(chosen, 1.0, 0.0).astype(jnp.bfloat16))
    hidden_copy.wait()
    blocks = [
        jnp.dot(choices[k], hidden[k], preferred_element_type=jnp.float32).astype(jnp.bfloat16)
        for k in range(steps)
    ]
    left = jnp.concatenate(blocks, axis=1)
    for part in range(CHUNKS):
        fetches[part].wait()
        right = grads[part].reshape(steps * tokens, width)
        product = jnp.dot(left, right, preferred_element_type=jnp.float32)
        out_ref[:, :, part * width : (part + 1) * width] = product.reshape(rings, group, width)


def partial_gradients(hidden_acts, out_grads, rings):
    steps, rows, tokens = hidden_acts.shape
    columns = out_grads.shape[2]
    return pl.pallas_call(
        functools.partial(partial_kernel, rings),
        out_shape=jax.ShapeDtypeStruct((rings, steps * rows // rings, columns), jnp.float32),
        in_specs=[pl.BlockSpec(memory_space=pltpu.HBM)] * 2,
        out_specs=pl.BlockSpec(memory_space=pltpu.VMEM),
        scratch_shapes=[
            pltpu.VMEM(hidden_acts.shape, hidden_acts.dtype),
            pltpu.VMEM((CHUNKS, steps, tokens, columns // CHUNKS), out_grads.dtype),
            pltpu.SemaphoreType.DMA,
            pltpu.SemaphoreType.DMA((CHUNKS,)),
        ],
        compiler_params=pltpu.CompilerParams(vmem_limit_bytes=24 * 1024 * 1024),
        name="partial_gradients",
    )(
        pltpu.with_memory_space_constraint(hidden_acts, pltpu.HBM),
        pltpu.with_memory_space_constraint(out_grads, pltpu.HBM),
    )


def reduce_line(parts):
    size = lax.axis_size("dp")
    place = lax.axis_index("dp")
    at = lambda shift: pick(parts, lax.rem(place + shift + 2 * size, size))
    end = size - 1
    last = size - 2
    rights = [(k, k + 1) for k in range(end)]
    lefts = [(k + 1, k) for k in range(end)]
    up_sent = at(jnp.where(place == 0, end, 1))
    down_sent = at(jnp.where(place == end, -end, -1))
    up = lax.ppermute(up_sent, "dp", rights)
    down = lax.ppermute(down_sent, "dp", lefts)
    near = jnp.where(place >= 2, up, 0.0) + jnp.where(place <= end - 2, down, 0.0)
    own = at(0) + near
    for step in range(2, last):
        up, _ = lax.optimization_barrier((up, down_sent))
        up_sent = at(-step) + up
        if step == 4:
            up_sent, own = lax.optimization_barrier((up_sent, own))
        up = lax.ppermute(up_sent, "dp", [(k, k + 1) for k in range(step)])
        down, _ = lax.optimization_barrier((down, up_sent))
        down_sent = at(step) + down
        down = lax.ppermute(down_sent, "dp", [(end - k, end - k - 1) for k in range(step)])
        if step == 5:
            edge, _ = lax.optimization_barrier((at(jnp.where(place == 0, 1, -1)), down_sent))
            edge = lax.ppermute(edge, "dp", [(0, 1), (end, end - 1)])
    up, _ = lax.optimization_barrier((up, down_sent))
    up_sent = at(2) + up
    up = lax.ppermute(up_sent, "dp", [(k, k + 2) for k in range(last)])
    down, _ = lax.optimization_barrier((down, up_sent))
    down_sent = at(-2) + down
    down = lax.ppermute(down_sent, "dp", [(k + 2, k) for k in range(last)])
    return (up + down) + (own + edge)


def copies(block, count):
    return jnp.broadcast_to(block[None], (count,) + block.shape)


def body(
    local_weight, adam_first, adam_second, hidden_acts, out_grads, global_weight, outer_momentum
):
    replicas = 1
    for size in REPLICA_PARTS.values():
        replicas *= size
    inner = REPLICA_PARTS["x"] * REPLICA_PARTS["core"]
    outer = replicas // inner
    rings = lax.axis_size("dp")
    steps_count = hidden_acts.shape[0]
    row_total, columns = local_weight.shape
    summed = reduce_line(partial_gradients(hidden_acts, out_grads, rings))

    weight = local_weight
    first_moment = adam_first
    second_moment = adam_second
    for k in range(steps_count):
        gradient = summed[k * row_total : (k + 1) * row_total]
        first_moment = beta_one * first_moment + (1.0 - beta_one) * gradient
        second_moment = beta_two * second_moment + (1.0 - beta_two) * gradient * gradient
        update = first_moment / (jnp.sqrt(second_moment) + tiny_eps)
        weight = weight - inner_rate * (update + decay_rate * weight)

    pull = outer_rate * (1.0 + outer_beta)
    still = global_weight - pull * global_weight - outer_rate * outer_beta * outer_beta * outer_momentum
    far = lax.axis_index("far")
    sides = REPLICA_PARTS["far"]
    lines = REPLICA_PARTS["y"]
    parts = weight.reshape(row_total, lines, sides, inner, LANES).transpose(1, 3, 2, 0, 4)
    parts = parts.reshape((lines * inner, sides) + still.shape)
    mine = lax.broadcasted_iota(jnp.int32, parts.shape[1:], 0) == far
    added = jnp.where(mine, still[None], 0.0)
    parts, added, still, far = lax.optimization_barrier((parts, added, still, far))
    parts = lax.all_to_all(parts, ("y", "x", "core"), 0, 0, tiled=True)
    share = jnp.sum(parts, axis=0) * (pull / replicas) + added
    known = share + lax.ppermute(share, "far", [(0, 1), (1, 0)])
    new_global = pick(known, far)
    average = (new_global - still) * (1.0 / pull)
    new_momentum = outer_beta * outer_momentum + (global_weight - average)
    sent, new_global, new_momentum = lax.optimization_barrier(
        (copies(known, lines * inner), new_global, new_momentum)
    )
    gathered = lax.all_to_all(sent, ("y", "x", "core"), 0, 0, tiled=True)
    gathered = gathered.reshape((lines, inner, sides) + still.shape)
    gathered = gathered.transpose(3, 0, 2, 1, 4).reshape(row_total, columns)
    new_local = mix_share * weight + (1.0 - mix_share) * gathered
    return (new_local, first_moment, second_moment, new_global, new_momentum)


def solution(mesh):
    sizes = tuple(REPLICA_PARTS.values()) + (mesh.shape["dp"],)
    fine = Mesh(mesh.devices.reshape(sizes), tuple(REPLICA_PARTS) + ("dp",))
    replica = tuple(REPLICA_PARTS)
    stacked = P(replica + ("dp",), None)
    held = P("dp", replica)
    return jax.shard_map(
        body,
        mesh=fine,
        in_specs=(
            stacked,
            stacked,
            stacked,
            P(None, None, replica + ("dp",)),
            P(None, replica + ("dp",), None),
            held,
            held,
        ),
        out_specs=(stacked, stacked, stacked, held, held),
        check_vma=False,
    )
```

```python
import functools

import jax
import jax.numpy as jnp
from jax import lax
from jax.experimental import pallas as pl
from jax.experimental.pallas import tpu as pltpu
from jax.sharding import Mesh
from jax.sharding import PartitionSpec as P

beta_one = 0.9
beta_two = 0.95
inner_rate = 0.02
decay_rate = 0.1
tiny_eps = 1e-08
outer_rate = 0.7
outer_beta = 0.9
mix_share = 0.5

REPLICA_PARTS = {"y": 4, "far": 2, "x": 4, "core": 2}
OUTER = ("y", "far")
INNER = ("x", "core")
LANES = 128


def pick(parts, index):
    return lax.dynamic_index_in_dim(parts, index, 0, keepdims=False)


CHUNKS = 2


def partial_kernel(rings, hidden_hbm, grads_hbm, out_ref, hidden, grads, hidden_sem, grads_sem):
    steps, rows, tokens = hidden.shape
    width = grads.shape[3]
    held = rows // rings
    group = steps * held
    total = rings * group
    hidden_copy = pltpu.make_async_copy(hidden_hbm, hidden, hidden_sem)
    hidden_copy.start()
    fetches = []
    for part in range(CHUNKS):
        fetch = pltpu.make_async_copy(
            grads_hbm.at[:, :, pl.ds(part * width, width)], grads.at[part], grads_sem.at[part]
        )
        fetch.start()
        fetches.append(fetch)
    place = lax.broadcasted_iota(jnp.int32, (total, rows), 0)
    source = lax.broadcasted_iota(jnp.int32, (total, rows), 1)
    choices = []
    for k in range(steps):
        wanted = (place // group) * held + place % group - k * held
        chosen = (source == wanted) & ((place % group) // held == k)
        choices.append(jnp.where(chosen, 1.0, 0.0).astype(jnp.bfloat16))
    hidden_copy.wait()
    blocks = [
        jnp.dot(choices[k], hidden[k], preferred_element_type=jnp.float32).astype(jnp.bfloat16)
        for k in range(steps)
    ]
    left = jnp.concatenate(blocks, axis=1)
    for part in range(CHUNKS):
        fetches[part].wait()
        right = grads[part].reshape(steps * tokens, width)
        product = jnp.dot(left, right, preferred_element_type=jnp.float32)
        out_ref[:, :, part * width : (part + 1) * width] = product.reshape(rings, group, width)


def partial_gradients(hidden_acts, out_grads, rings):
    steps, rows, tokens = hidden_acts.shape
    columns = out_grads.shape[2]
    return pl.pallas_call(
        functools.partial(partial_kernel, rings),
        out_shape=jax.ShapeDtypeStruct((rings, steps * rows // rings, columns), jnp.float32),
        in_specs=[pl.BlockSpec(memory_space=pltpu.HBM)] * 2,
        out_specs=pl.BlockSpec(memory_space=pltpu.VMEM),
        scratch_shapes=[
            pltpu.VMEM(hidden_acts.shape, hidden_acts.dtype),
            pltpu.VMEM((CHUNKS, steps, tokens, columns // CHUNKS), out_grads.dtype),
            pltpu.SemaphoreType.DMA,
            pltpu.SemaphoreType.DMA((CHUNKS,)),
        ],
        compiler_params=pltpu.CompilerParams(vmem_limit_bytes=24 * 1024 * 1024),
        name="partial_gradients",
    )(
        pltpu.with_memory_space_constraint(hidden_acts, pltpu.HBM),
        pltpu.with_memory_space_constraint(out_grads, pltpu.HBM),
    )


def reduce_line(parts):
    size = lax.axis_size("dp")
    place = lax.axis_index("dp")
    at = lambda shift: pick(parts, lax.rem(place + shift + 2 * size, size))
    end = size - 1
    last = size - 2
    rights = [(k, k + 1) for k in range(end)]
    lefts = [(k + 1, k) for k in range(end)]
    up_sent = at(jnp.where(place == 0, end, 1))
    down_sent = at(jnp.where(place == end, -end, -1))
    up = lax.ppermute(up_sent, "dp", rights)
    down = lax.ppermute(down_sent, "dp", lefts)
    near = jnp.where(place >= 2, up, 0.0) + jnp.where(place <= end - 2, down, 0.0)
    own = at(0) + near
    for step in range(2, last):
        up, _ = lax.optimization_barrier((up, down_sent))
        up_sent = at(-step) + up
        if step == 4:
            up_sent, own = lax.optimization_barrier((up_sent, own))
        up = lax.ppermute(up_sent, "dp", [(k, k + 1) for k in range(step)])
        down, _ = lax.optimization_barrier((down, up_sent))
        down_sent = at(step) + down
        down = lax.ppermute(down_sent, "dp", [(end - k, end - k - 1) for k in range(step)])
        if step == 5:
            edge, _ = lax.optimization_barrier((at(jnp.where(place == 0, 1, -1)), down_sent))
            edge = lax.ppermute(edge, "dp", [(0, 1), (end, end - 1)])
    up, _ = lax.optimization_barrier((up, down_sent))
    up_sent = at(2) + up
    up = lax.ppermute(up_sent, "dp", [(k, k + 2) for k in range(last)])
    down, _ = lax.optimization_barrier((down, up_sent))
    down_sent = at(-2) + down
    down = lax.ppermute(down_sent, "dp", [(k + 2, k) for k in range(last)])
    return (up + down) + (own + edge)


def copies(block, count):
    return jnp.broadcast_to(block[None], (count,) + block.shape)


def body(
    local_weight, adam_first, adam_second, hidden_acts, out_grads, global_weight, outer_momentum
):
    replicas = 1
    for size in REPLICA_PARTS.values():
        replicas *= size
    inner = REPLICA_PARTS["x"] * REPLICA_PARTS["core"]
    outer = replicas // inner
    rings = lax.axis_size("dp")
    steps_count = hidden_acts.shape[0]
    row_total, columns = local_weight.shape
    summed = reduce_line(partial_gradients(hidden_acts, out_grads, rings))

    weight = local_weight
    first_moment = adam_first
    second_moment = adam_second
    for k in range(steps_count):
        gradient = summed[k * row_total : (k + 1) * row_total]
        first_moment = beta_one * first_moment + (1.0 - beta_one) * gradient
        second_moment = beta_two * second_moment + (1.0 - beta_two) * gradient * gradient
        update = first_moment / (jnp.sqrt(second_moment) + tiny_eps)
        weight = weight - inner_rate * (update + decay_rate * weight)

    pull = outer_rate * (1.0 + outer_beta)
    still = global_weight - pull * global_weight - outer_rate * outer_beta * outer_beta * outer_momentum
    far = lax.axis_index("far")
    sides = REPLICA_PARTS["far"]
    lines = REPLICA_PARTS["y"]
    grid = (row_total, lines, sides, REPLICA_PARTS["x"], REPLICA_PARTS["core"], LANES)
    parts = weight.reshape(grid).transpose((3, 1, 4, 2, 0, 5))
    parts = parts.reshape((lines * inner, sides) + still.shape)
    mine = lax.broadcasted_iota(jnp.int32, parts.shape[1:], 0) == far
    added = jnp.where(mine, still[None], 0.0)
    parts, added, still, far = lax.optimization_barrier((parts, added, still, far))
    parts = lax.all_to_all(parts, ("x", "y", "core"), 0, 0, tiled=True)
    share = jnp.sum(parts, axis=0) * (pull / replicas) + added
    known = share + lax.ppermute(share, "far", [(0, 1), (1, 0)])
    new_global = pick(known, far)
    average = (new_global - still) * (1.0 / pull)
    new_momentum = outer_beta * outer_momentum + (global_weight - average)
    sent, new_global, new_momentum = lax.optimization_barrier(
        (copies(known, lines * inner), new_global, new_momentum)
    )
    gathered = lax.all_to_all(sent, ("x", "y", "core"), 0, 0, tiled=True)
    gathered = gathered.reshape(tuple(grid[k] for k in (3, 1, 4, 2, 0, 5)))
    gathered = gathered.transpose((4, 1, 3, 0, 2, 5)).reshape(row_total, columns)
    new_local = mix_share * weight + (1.0 - mix_share) * gathered
    return (new_local, first_moment, second_moment, new_global, new_momentum)


def solution(mesh):
    sizes = tuple(REPLICA_PARTS.values()) + (mesh.shape["dp"],)
    fine = Mesh(mesh.devices.reshape(sizes), tuple(REPLICA_PARTS) + ("dp",))
    replica = tuple(REPLICA_PARTS)
    stacked = P(replica + ("dp",), None)
    held = P("dp", replica)
    return jax.shard_map(
        body,
        mesh=fine,
        in_specs=(
            stacked,
            stacked,
            stacked,
            P(None, None, replica + ("dp",)),
            P(None, replica + ("dp",), None),
            held,
            held,
        ),
        out_specs=(stacked, stacked, stacked, held, held),
        check_vma=False,
    )
```

```python
import functools

import jax
import jax.numpy as jnp
from jax import lax
from jax.experimental import pallas as pl
from jax.experimental.pallas import tpu as pltpu
from jax.sharding import Mesh
from jax.sharding import PartitionSpec as P

beta_one = 0.9
beta_two = 0.95
inner_rate = 0.02
decay_rate = 0.1
tiny_eps = 1e-08
outer_rate = 0.7
outer_beta = 0.9
mix_share = 0.5

REPLICA_PARTS = {"y": 4, "far": 2, "x": 4, "core": 2}
OUTER = ("y", "far")
INNER = ("x", "core")
LANES = 128


def pick(parts, index):
    return lax.dynamic_index_in_dim(parts, index, 0, keepdims=False)


CHUNKS = 2


def partial_kernel(rings, hidden_hbm, grads_hbm, out_ref, hidden, grads, hidden_sem, grads_sem):
    steps, rows, tokens = hidden.shape
    width = grads.shape[3]
    held = rows // rings
    group = steps * held
    total = rings * group
    hidden_copy = pltpu.make_async_copy(hidden_hbm, hidden, hidden_sem)
    hidden_copy.start()
    fetches = []
    for part in range(CHUNKS):
        fetch = pltpu.make_async_copy(
            grads_hbm.at[:, :, pl.ds(part * width, width)], grads.at[part], grads_sem.at[part]
        )
        fetch.start()
        fetches.append(fetch)
    place = lax.broadcasted_iota(jnp.int32, (total, rows), 0)
    source = lax.broadcasted_iota(jnp.int32, (total, rows), 1)
    choices = []
    for k in range(steps):
        wanted = (place // group) * held + place % group - k * held
        chosen = (source == wanted) & ((place % group) // held == k)
        choices.append(jnp.where(chosen, 1.0, 0.0).astype(jnp.bfloat16))
    hidden_copy.wait()
    blocks = [
        jnp.dot(choices[k], hidden[k], preferred_element_type=jnp.float32).astype(jnp.bfloat16)
        for k in range(steps)
    ]
    left = jnp.concatenate(blocks, axis=1)
    for part in range(CHUNKS):
        fetches[part].wait()
        right = grads[part].reshape(steps * tokens, width)
        product = jnp.dot(left, right, preferred_element_type=jnp.float32)
        out_ref[:, :, part * width : (part + 1) * width] = product.reshape(rings, group, width)


def partial_gradients(hidden_acts, out_grads, rings):
    steps, rows, tokens = hidden_acts.shape
    columns = out_grads.shape[2]
    return pl.pallas_call(
        functools.partial(partial_kernel, rings),
        out_shape=jax.ShapeDtypeStruct((rings, steps * rows // rings, columns), jnp.float32),
        in_specs=[pl.BlockSpec(memory_space=pltpu.HBM)] * 2,
        out_specs=pl.BlockSpec(memory_space=pltpu.VMEM),
        scratch_shapes=[
            pltpu.VMEM(hidden_acts.shape, hidden_acts.dtype),
            pltpu.VMEM((CHUNKS, steps, tokens, columns // CHUNKS), out_grads.dtype),
            pltpu.SemaphoreType.DMA,
            pltpu.SemaphoreType.DMA((CHUNKS,)),
        ],
        compiler_params=pltpu.CompilerParams(vmem_limit_bytes=24 * 1024 * 1024),
        name="partial_gradients",
    )(
        pltpu.with_memory_space_constraint(hidden_acts, pltpu.HBM),
        pltpu.with_memory_space_constraint(out_grads, pltpu.HBM),
    )


def reduce_line(parts):
    size = lax.axis_size("dp")
    place = lax.axis_index("dp")
    at = lambda shift: pick(parts, lax.rem(place + shift + 2 * size, size))
    end = size - 1
    last = size - 2
    rights = [(k, k + 1) for k in range(end)]
    lefts = [(k + 1, k) for k in range(end)]
    up_sent = at(jnp.where(place == 0, end, 1))
    down_sent = at(jnp.where(place == end, -end, -1))
    up = lax.ppermute(up_sent, "dp", rights)
    down = lax.ppermute(down_sent, "dp", lefts)
    near = jnp.where(place >= 2, up, 0.0) + jnp.where(place <= end - 2, down, 0.0)
    own = at(0) + near
    for step in range(2, last):
        up, _ = lax.optimization_barrier((up, down_sent))
        up_sent = at(-step) + up
        if step == 4:
            up_sent, own = lax.optimization_barrier((up_sent, own))
        up = lax.ppermute(up_sent, "dp", [(k, k + 1) for k in range(step)])
        down, _ = lax.optimization_barrier((down, up_sent))
        down_sent = at(step) + down
        down = lax.ppermute(down_sent, "dp", [(end - k, end - k - 1) for k in range(step)])
    up, _ = lax.optimization_barrier((up, down_sent))
    up_sent = at(2) + up
    up = lax.ppermute(up_sent, "dp", [(k, k + 2) for k in range(last)])
    down, _ = lax.optimization_barrier((down, up_sent))
    down_sent = at(-2) + down
    down = lax.ppermute(down_sent, "dp", [(k + 2, k) for k in range(last)])
    edge = at(jnp.where(place == 0, 1, -1))
    edge, _ = lax.optimization_barrier((edge, down_sent))
    edge = lax.ppermute(edge, "dp", [(0, 1), (end, end - 1)])
    return (up + down) + (own + edge)


def copies(block, count):
    return jnp.broadcast_to(block[None], (count,) + block.shape)


def body(
    local_weight, adam_first, adam_second, hidden_acts, out_grads, global_weight, outer_momentum
):
    replicas = 1
    for size in REPLICA_PARTS.values():
        replicas *= size
    inner = REPLICA_PARTS["x"] * REPLICA_PARTS["core"]
    outer = replicas // inner
    rings = lax.axis_size("dp")
    steps_count = hidden_acts.shape[0]
    row_total, columns = local_weight.shape
    summed = reduce_line(partial_gradients(hidden_acts, out_grads, rings))

    weight = local_weight
    first_moment = adam_first
    second_moment = adam_second
    for k in range(steps_count):
        gradient = summed[k * row_total : (k + 1) * row_total]
        first_moment = beta_one * first_moment + (1.0 - beta_one) * gradient
        second_moment = beta_two * second_moment + (1.0 - beta_two) * gradient * gradient
        update = first_moment / (jnp.sqrt(second_moment) + tiny_eps)
        weight = weight - inner_rate * (update + decay_rate * weight)

    pull = outer_rate * (1.0 + outer_beta)
    still = global_weight - pull * global_weight - outer_rate * outer_beta * outer_beta * outer_momentum
    far = lax.axis_index("far")
    sides = REPLICA_PARTS["far"]
    lines = REPLICA_PARTS["y"]
    parts = weight.reshape(row_total, lines, sides, inner, LANES).transpose(1, 3, 2, 0, 4)
    parts = parts.reshape((lines * inner, sides) + still.shape)
    mine = lax.broadcasted_iota(jnp.int32, parts.shape[1:], 0) == far
    added = jnp.where(mine, still[None], 0.0)
    parts, added, still, far = lax.optimization_barrier((parts, added, still, far))
    parts = lax.all_to_all(parts, ("y", "x", "core"), 0, 0, tiled=True)
    share = jnp.sum(parts, axis=0) * (pull / replicas) + added
    known = share + lax.ppermute(share, "far", [(0, 1), (1, 0)])
    new_global = pick(known, far)
    average = (new_global - still) * (1.0 / pull)
    new_momentum = outer_beta * outer_momentum + (global_weight - average)
    sent, new_global, new_momentum = lax.optimization_barrier(
        (copies(known, lines * inner), new_global, new_momentum)
    )
    gathered = lax.all_to_all(sent, ("y", "x", "core"), 0, 0, tiled=True)
    gathered = gathered.reshape((lines, inner, sides) + still.shape)
    gathered = gathered.transpose(3, 0, 2, 1, 4).reshape(row_total, columns)
    new_local = mix_share * weight + (1.0 - mix_share) * gathered
    return (new_local, first_moment, second_moment, new_global, new_momentum)


def solution(mesh):
    sizes = tuple(REPLICA_PARTS.values()) + (mesh.shape["dp"],)
    fine = Mesh(mesh.devices.reshape(sizes), tuple(REPLICA_PARTS) + ("dp",))
    replica = tuple(REPLICA_PARTS)
    stacked = P(replica + ("dp",), None)
    held = P("dp", replica)
    return jax.shard_map(
        body,
        mesh=fine,
        in_specs=(
            stacked,
            stacked,
            stacked,
            P(None, None, replica + ("dp",)),
            P(None, replica + ("dp",), None),
            held,
            held,
        ),
        out_specs=(stacked, stacked, stacked, held, held),
        check_vma=False,
    )
```
